32 devices in a mesh: slab: 4 (over y, x), expert: 8 (over z, core).
Axes of the slice: x: 2, y: 2, z: 4, core: 2. Of those that a mesh axis runs over, the one named last changes fastest.
Arguments:
- features: bfloat16 [8, 32, 64, 1024], P('expert', 'slab'), may hold values from -6 to 6
- expert_ids: int32 [8, 32, 64, 2], P('expert', 'slab'), may hold values from 0 to 7, as said below
- positions: int32 [8, 32, 64, 2], P('expert', 'slab'), may hold values from 0 to 511, as said below
- gates: float32 [8, 32, 64, 2], P('expert', 'slab'), may hold values from 0.2 to 1
- w_in: bfloat16 [8, 1024, 4096], P('expert'), may hold values from -0.1875 to 0.1875
- w_out: bfloat16 [8, 4096, 1024], P('expert'), may hold values from -0.09375 to 0.09375
- w_proj: bfloat16 [1024, 256], replicated, may hold values from -0.1875 to 0.1875
- kernel_one: bfloat16 [3, 3, 256, 256], replicated, may hold values from -0.125 to 0.125
- kernel_two: bfloat16 [3, 3, 256, 256], replicated, may hold values from -0.125 to 0.125
Outputs:
- joined: bfloat16 [8, 32, 64, 256], P('expert', 'slab')
The draws below stay inside these ranges and needn't reach their ends.
Inputs may be any that keep to these rules, and one draw needn't show every extreme that they name: `expert_ids`: the two experts of a token differ. Within one band, the assignments to one expert hold the positions 0, 1, 2, ... each once.
All inputs are finite; a program needn't handle non-finite values.
Results may differ from the reference program's by a relative error of at most 0.009.
Values may be sent and summed in bfloat16 or wider, within the bound.
A program may use at most 128 MiB of HBM per device.

```python
import jax
import jax.numpy as jnp
from jax import lax

D = 1024
HID = 4096
CH = 256
COLS = 64
ROWS_DEV = 8
EXPERTS = 8
CAP = 192
MAPS = 8
ROWS = 32
N_SLAB = 4


def pick_expert(pick_key, ticket_edges, token_count):
    tickets = jax.random.randint(pick_key, (token_count,), 0, ticket_edges[-1])
    return jnp.sum((tickets[:, None] >= ticket_edges[None, :]).astype(jnp.int32), axis=1).astype(jnp.int32)


def assignments(key):
    base_key = jax.random.fold_in(key, 41)
    k_weight, k_first, k_second, k_offset, k_order, k_hot = jax.random.split(base_key, 6)
    expert_weights = jax.random.randint(k_weight, (EXPERTS,), 1, 9)
    ticket_edges = jnp.cumsum(expert_weights).astype(jnp.int32)
    token_count = MAPS * ROWS * COLS
    band_tokens = ROWS_DEV * COLS
    first_pick = pick_expert(k_first, ticket_edges, token_count)
    hot_expert = jax.random.randint(k_hot, (), 0, EXPERTS).astype(jnp.int32)
    token_number = jnp.arange(token_count)
    first_pick = jnp.where(token_number < band_tokens, hot_expert, first_pick).astype(jnp.int32)
    second_pick = pick_expert(k_second, ticket_edges, token_count)
    offset_draw = jax.random.randint(k_offset, (token_count,), 1, EXPERTS)
    second_pick = jnp.where(second_pick == first_pick, (first_pick + offset_draw) % EXPERTS, second_pick)
    pair_ids = jnp.stack([first_pick, second_pick], axis=1).astype(jnp.int32)
    sources = MAPS * (ROWS // ROWS_DEV)
    per_source = 2 * band_tokens
    flat_ids = pair_ids.reshape(sources, per_source)
    block_keys = jax.random.split(k_order, sources)

    def rank_block(block_key, block_ids):
        priority = jax.random.permutation(block_key, per_source)
        sorted_ids = block_ids[priority]
        one_hot = (sorted_ids[:, None] == jnp.arange(EXPERTS)[None, :]).astype(jnp.int32)
        earlier = jnp.cumsum(one_hot, axis=0) - one_hot
        ranking = jnp.sum(earlier * one_hot, axis=1).astype(jnp.int32)
        return jnp.zeros((per_source,), jnp.int32).at[priority].set(ranking)
    slot_pos = jax.vmap(rank_block)(block_keys, flat_ids)
    return (pair_ids.reshape(MAPS, ROWS, COLS, 2), slot_pos.reshape(MAPS, ROWS, COLS, 2))


def draw_expert_ids(key, part):
    return assignments(key)[0]


def draw_positions(key, part):
    return assignments(key)[1]


def block_levels(key, shape, cuts, least, largest):
    gain, own = 1.0, jax.random.fold_in(key, 6)
    for position, blocks in cuts:
        heights = jnp.exp(jax.random.uniform(jax.random.fold_in(own, position), (blocks,), jnp.float32, least / len(cuts), largest / len(cuts)))
        gain = gain * jnp.repeat(heights, shape[position] // blocks).reshape([-1 if axis == position else 1 for axis in range(len(shape))])
    return gain


def scatter_about(own_key, extent, width, bound, cuts=(), dtype=jnp.bfloat16):
    gain = block_levels(own_key, extent, cuts, -0.22, 0.18) if cuts else 1.0
    result = jax.random.normal(own_key, extent, jnp.float32) * width * gain
    return jnp.minimum(jnp.maximum(result, -bound), bound).astype(dtype)


def setup_inputs(seed: int = 0) -> dict:
    streams_of = jax.random.split(jax.random.key(seed), 10)
    features = scatter_about(streams_of[0], (MAPS, ROWS, COLS, D), 1.0, 6.0, ((0, 8), (1, 4)))
    expert_ids = draw_expert_ids(jax.random.fold_in(streams_of[9], 71), 0)
    positions = draw_positions(jax.random.fold_in(streams_of[9], 71), 0)
    gates = jnp.clip(0.2 + 0.8 * jax.random.uniform(streams_of[3], (MAPS, ROWS, COLS, 2), jnp.float32) ** block_levels(streams_of[3], (MAPS, ROWS, COLS, 2), ((0, 8), (1, 4)), -0.2, 0.2), 0.2, 1.0)
    w_in = scatter_about(streams_of[4], (EXPERTS, D, HID), D ** -0.5, 0.1875, ((0, 8),))
    w_out = scatter_about(streams_of[5], (EXPERTS, HID, D), HID ** -0.5, 0.09375, ((0, 8),))
    w_proj = scatter_about(streams_of[6], (D, CH), D ** -0.5, 0.1875)
    kernel_one = scatter_about(streams_of[7], (3, 3, CH, CH), (9 * CH) ** -0.5, 0.125)
    kernel_two = scatter_about(streams_of[8], (3, 3, CH, CH), (9 * CH) ** -0.5, 0.125)
    return {"features": features, "expert_ids": expert_ids, "positions": positions, "gates": gates, "w_in": w_in, "w_out": w_out, "w_proj": w_proj, "kernel_one": kernel_one, "kernel_two": kernel_two}


def conv_rows(padded, kernel):
    out_rows = padded.shape[0] - 2
    width_cols = padded.shape[1]
    channels = padded.shape[2]
    widened = jnp.pad(padded, ((0, 0), (1, 1), (0, 0)))
    columns = jnp.concatenate([widened[:, 0:width_cols], widened[:, 1:width_cols + 1], widened[:, 2:width_cols + 2]], axis=-1)
    kernel_taps = kernel.reshape(3, 3 * channels, -1)
    total = jnp.zeros((out_rows * width_cols, kernel.shape[3]), jnp.float32)
    for row_shift in range(3):
        window = columns[row_shift:row_shift + out_rows].reshape(out_rows * width_cols, 3 * channels)
        total = total + jnp.dot(window, kernel_taps[row_shift], preferred_element_type=jnp.float32)
    return total.reshape(out_rows, width_cols, -1)

def reference(features, expert_ids, positions, gates, w_in, w_out, w_proj, kernel_one, kernel_two):
    sources = MAPS * N_SLAB
    tokens_band = ROWS_DEV * COLS
    resident = features.reshape(sources, tokens_band, D)
    slot_ids = expert_ids.reshape(sources, 2 * tokens_band)
    slot_pos = positions.reshape(sources, 2 * tokens_band)
    gate_vals = gates.reshape(sources, 2 * tokens_band)
    wide32 = resident.astype(jnp.float32)
    normed = (wide32 * lax.rsqrt(lax.optimization_barrier(jnp.mean(wide32 * wide32, axis=-1, keepdims=True)) + 1e-06)).astype(jnp.bfloat16)
    usable = slot_pos < CAP
    slot_index = jnp.where(usable, slot_ids * CAP + slot_pos, EXPERTS * CAP).astype(jnp.int32)
    token_rows = jnp.repeat(normed, 2, axis=1)

    def fill_band(index_band, rows_band):
        empty = jnp.zeros((EXPERTS * CAP, D), jnp.bfloat16)
        return empty.at[index_band].set(rows_band, mode='drop')
    buffers = jax.vmap(fill_band)(slot_index, token_rows).reshape(sources, EXPERTS, CAP, D)
    by_expert = jnp.swapaxes(buffers, 0, 1)

    def run_expert(packed):
        block_rows, weight_in, weight_out = packed
        flat_rows = block_rows.reshape(sources * CAP, D)
        pre_act = jnp.dot(flat_rows, weight_in, preferred_element_type=jnp.float32)
        activation = jax.nn.gelu(pre_act).astype(jnp.bfloat16)
        expert_out = jnp.dot(activation, weight_out, preferred_element_type=jnp.float32).astype(jnp.bfloat16)
        return expert_out.reshape(sources, CAP, D)
    outputs = lax.map(run_expert, (by_expert, w_in, w_out))
    returned = jnp.swapaxes(outputs, 0, 1).reshape(sources, EXPERTS * CAP, D)
    fetch = jnp.where(usable, slot_index, 0).astype(jnp.int32)
    picked = jnp.take_along_axis(returned, fetch[:, :, None], axis=1)
    slot_proj = jnp.dot(picked.reshape(-1, D), w_proj, preferred_element_type=jnp.float32)
    base_proj = jnp.dot(resident.reshape(-1, D), w_proj, preferred_element_type=jnp.float32)
    weight_mix = jnp.where(usable, gate_vals, 0.0).reshape(sources, tokens_band, 2, 1)
    slot_terms = slot_proj.reshape(sources, tokens_band, 2, CH) * weight_mix
    neck_map = (base_proj.reshape(sources, tokens_band, CH) + lax.optimization_barrier(jnp.sum(slot_terms, axis=2))).astype(jnp.bfloat16)
    neck_map = neck_map.reshape(MAPS, ROWS, COLS, CH)
    padded_neck = jnp.pad(neck_map, ((0, 0), (1, 1), (0, 0), (0, 0)))
    first_conv = jax.vmap(lambda field: conv_rows(field, kernel_one))(padded_neck)
    hidden = jax.nn.gelu(first_conv).astype(jnp.bfloat16)
    padded_hidden = jnp.pad(hidden, ((0, 0), (1, 1), (0, 0), (0, 0)))
    second_conv = jax.vmap(lambda field: conv_rows(field, kernel_two))(padded_hidden)
    return (neck_map.astype(jnp.float32) + second_conv).astype(jnp.bfloat16)
```

```python
import functools

import jax
import jax.numpy as jnp
from jax import lax
from jax.experimental import pallas as pl
from jax.experimental.pallas import tpu as pltpu
from jax.sharding import PartitionSpec as P

MESH = pl.DeviceIdType.MESH
HIDDEN_TILE = 1024
FUSE_TILE = 512


def gelu(value):
    inner = 0.7978845608028654 * (value + 0.044715 * (value * value * value))
    half = 0.5 * value
    return half + half * jnp.tanh(inner)


def paired(me, step, count):
    partner, bit = 0, 1
    while bit < count:
        partner = partner + ((me // bit + step // bit) % 2) * bit
        bit *= 2
    return partner


def kernel(
    owners, slabs, capacity, rows, cols,
    features, codes_row, codes_col, gates, w_in_hbm, w_out_hbm, w_proj_hbm, one_hbm, two_hbm,
    joined,
    w_in, w_out, w_proj, one, two, fused, normed, sent, held, back, returned, total,
    neck, hidden, columns,
    load_sem, sent_sem, held_sem, back_sem, returned_sem, edge_sent, edge_held,
):
    me = lax.axis_index("expert")
    slab = lax.axis_index("slab")
    tokens, width = features.shape
    hidden_units = w_in.shape[1]
    loads = [
        pltpu.make_async_copy(source, target, load_sem.at[place])
        for place, (source, target) in enumerate(
            [(w_out_hbm.at[0], w_out), (w_proj_hbm, w_proj), (w_in_hbm.at[0], w_in),
             (one_hbm, one), (two_hbm, two)]
        )
    ]
    for load in loads:
        load.start()

    barrier = pltpu.get_barrier_semaphore()

    @pl.loop(1, owners)
    def _(step):
        pl.semaphore_signal(
            barrier, inc=1, device_id=(slab, paired(me, step, owners)), device_id_type=MESH
        )

    @pl.when(slab > 0)
    def _():
        pl.semaphore_signal(barrier, inc=1, device_id=(slab - 1, me), device_id_type=MESH)

    @pl.when(slab < slabs - 1)
    def _():
        pl.semaphore_signal(barrier, inc=1, device_id=(slab + 1, me), device_id_type=MESH)

    @pl.loop(0, tokens // cols)
    def _(chunk):
        piece = pl.ds(pl.multiple_of(chunk * cols, cols), cols)
        wide = features[piece, :].astype(jnp.float32)
        scale = lax.rsqrt(jnp.mean(wide * wide, axis=1, keepdims=True) + 1e-06)
        normed[piece, :] = (wide * scale).astype(jnp.bfloat16)

    neighbours = jnp.minimum(slab, 1) + jnp.minimum(slabs - 1 - slab, 1)
    pl.semaphore_wait(barrier, owners - 1 + neighbours)

    def dispatch(step):
        return pltpu.make_async_remote_copy(
            src_ref=sent.at[step], dst_ref=held.at[step],
            send_sem=sent_sem.at[step], recv_sem=held_sem.at[step],
            device_id=(slab, paired(me, step, owners)), device_id_type=MESH,
        )

    def giveback(step):
        return pltpu.make_async_remote_copy(
            src_ref=back.at[step], dst_ref=returned.at[step],
            send_sem=back_sem.at[step], recv_sem=returned_sem.at[step],
            device_id=(slab, paired(me, step, owners)), device_id_type=MESH,
        )

    def packed(step):
        slot = paired(me, step, owners) * capacity + lax.broadcasted_iota(
            jnp.int32, (capacity, tokens), 0
        )
        chosen = (codes_row[0:1, :] == slot) | (codes_row[1:2, :] == slot)
        choice = jnp.where(chosen, 1.0, 0.0).astype(jnp.bfloat16)
        return jnp.dot(choice, normed[...], preferred_element_type=jnp.float32).astype(jnp.bfloat16)

    @pl.loop(0, owners - 1)
    def _(turn):
        step = owners - 1 - turn
        sent[step] = packed(step)
        dispatch(step).start()

    held[0] = packed(0)

    loads[0].wait()
    loads[1].wait()

    @pl.loop(0, hidden_units // FUSE_TILE)
    def _(tile):
        piece = pl.ds(pl.multiple_of(tile * FUSE_TILE, FUSE_TILE), FUSE_TILE)
        fused[piece, :] = jnp.dot(
            w_out[piece, :], w_proj[...], preferred_element_type=jnp.float32
        ).astype(jnp.bfloat16)

    total[...] = jnp.dot(features[...], w_proj[...], preferred_element_type=jnp.float32)
    loads[2].wait()

    def expert(step):
        block = held[step]
        result = jnp.zeros((capacity, fused.shape[1]), jnp.float32)
        for tile in range(hidden_units // HIDDEN_TILE):
            piece = slice(tile * HIDDEN_TILE, (tile + 1) * HIDDEN_TILE)
            pre = jnp.dot(block, w_in[:, piece], preferred_element_type=jnp.float32)
            result = result + jnp.dot(
                gelu(pre).astype(jnp.bfloat16), fused[piece, :], preferred_element_type=jnp.float32
            )
        back[step] = result.astype(jnp.bfloat16)

    def combine(step, source):
        slot = paired(me, step, owners) * capacity + lax.broadcasted_iota(
            jnp.int32, (tokens, capacity), 1
        )
        outcome = source[step]
        for choice in range(2):
            chosen = codes_col[:, choice : choice + 1] == slot
            picked = jnp.dot(
                jnp.where(chosen, 1.0, 0.0).astype(jnp.bfloat16), outcome,
                preferred_element_type=jnp.float32,
            )
            total[...] += gates[:, choice : choice + 1] * picked

    @pl.loop(0, owners)
    def _(turn):
        step = (owners - turn) % owners

        @pl.when(step > 0)
        def _():
            dispatch(step).wait_recv()

        expert(step)

        @pl.when(step > 0)
        def _():
            giveback(step).start()

    combine(0, back)

    @pl.loop(0, owners - 1)
    def _(turn):
        step = owners - 1 - turn
        giveback(step).wait_recv()
        combine(step, returned)

    loads[3].wait()
    loads[4].wait()
    inside = slice(cols, cols + tokens)

    def edges(place, field):
        up = pltpu.make_async_remote_copy(
            src_ref=field.at[pl.ds(cols, cols)], dst_ref=field.at[pl.ds(cols + tokens, cols)],
            send_sem=edge_sent.at[place, 0], recv_sem=edge_held.at[place, 0],
            device_id=(jnp.maximum(slab - 1, 0), me), device_id_type=MESH,
        )
        down = pltpu.make_async_remote_copy(
            src_ref=field.at[pl.ds(tokens, cols)], dst_ref=field.at[pl.ds(0, cols)],
            send_sem=edge_sent.at[place, 1], recv_sem=edge_held.at[place, 1],
            device_id=(jnp.minimum(slab + 1, slabs - 1), me), device_id_type=MESH,
        )
        return up, down

    def spread(field, piece, count):
        centre = field[piece, :]
        channels = centre.shape[1]
        wide = centre.astype(jnp.float32)
        column = lax.broadcasted_iota(jnp.int32, (count, 1), 0) % cols
        columns[piece, 0:channels] = jnp.where(
            column == 0, 0.0, pltpu.roll(wide, 1, 0)
        ).astype(jnp.bfloat16)
        columns[piece, channels : 2 * channels] = centre
        columns[piece, 2 * channels : 3 * channels] = jnp.where(
            column == cols - 1, 0.0, pltpu.roll(wide, count - 1, 0)
        ).astype(jnp.bfloat16)

    def convolved(place, field, taps):
        up, down = edges(place, field)

        @pl.when(slab > 0)
        def _():
            up.start()

        @pl.when(slab < slabs - 1)
        def _():
            down.start()

        @pl.when(slab == 0)
        def _():
            field[0:cols, :] = jnp.zeros((cols, field.shape[1]), jnp.bfloat16)

        @pl.when(slab == slabs - 1)
        def _():
            field[cols + tokens :, :] = jnp.zeros((cols, field.shape[1]), jnp.bfloat16)

        spread(field, inside, tokens)
        total[...] = jnp.dot(columns[inside, :], taps[1], preferred_element_type=jnp.float32)

        @pl.when(slab > 0)
        def _():
            down.wait_recv()

        @pl.when(slab < slabs - 1)
        def _():
            up.wait_recv()

        spread(field, slice(0, cols), cols)
        spread(field, slice(cols + tokens, 2 * cols + tokens), cols)
        return (
            total[...]
            + jnp.dot(columns[0:tokens, :], taps[0], preferred_element_type=jnp.float32)
            + jnp.dot(
                columns[2 * cols : 2 * cols + tokens, :], taps[2],
                preferred_element_type=jnp.float32,
            )
        )

    neck[inside, :] = total[...].astype(jnp.bfloat16)
    hidden[inside, :] = gelu(convolved(0, neck, one)).astype(jnp.bfloat16)
    joined[...] = (
        neck[inside, :].astype(jnp.float32) + convolved(1, hidden, two)
    ).astype(jnp.bfloat16)

    @pl.loop(1, owners)
    def _(step):
        dispatch(step).wait_send()
        giveback(step).wait_send()

    for place, field in enumerate((neck, hidden)):
        up, down = edges(place, field)

        @pl.when(slab > 0)
        def _():
            up.wait_send()

        @pl.when(slab < slabs - 1)
        def _():
            down.wait_send()


def shards(owners, slabs, features, expert_ids, positions, gates, w_in, w_out, w_proj, kernel_one,
           kernel_two):
    maps_dev, rows_dev, width_cols, model_width = features.shape
    tokens_dev = maps_dev * rows_dev * width_cols
    local_experts, _, hidden_units = w_in.shape
    capacity = 3 * tokens_dev // (owners * local_experts)
    channels = w_proj.shape[1]
    codes = jnp.where(positions < capacity, expert_ids * capacity + positions, -1)
    codes = codes.reshape(tokens_dev, 2)
    vmem = pl.BlockSpec(memory_space=pltpu.VMEM)
    anywhere = pl.BlockSpec(memory_space=pl.ANY)
    bf16, f32 = jnp.bfloat16, jnp.float32
    padded = tokens_dev + 2 * width_cols
    joined = pl.pallas_call(
        functools.partial(kernel, owners, slabs, capacity, rows_dev, width_cols),
        out_shape=jax.ShapeDtypeStruct((tokens_dev, channels), bf16),
        in_specs=[vmem] * 4 + [anywhere] * 5,
        out_specs=vmem,
        scratch_shapes=[
            pltpu.VMEM((model_width, hidden_units), bf16),
            pltpu.VMEM((hidden_units, model_width), bf16),
            pltpu.VMEM((model_width, channels), bf16),
            pltpu.VMEM((3, 3 * channels, channels), bf16),
            pltpu.VMEM((3, 3 * channels, channels), bf16),
            pltpu.VMEM((hidden_units, channels), bf16),
            pltpu.VMEM((tokens_dev, model_width), bf16),
            pltpu.VMEM((owners, capacity, model_width), bf16),
            pltpu.VMEM((owners, capacity, model_width), bf16),
            pltpu.VMEM((owners, capacity, channels), bf16),
            pltpu.VMEM((owners, capacity, channels), bf16),
            pltpu.VMEM((tokens_dev, channels), f32),
            pltpu.VMEM((padded, channels), bf16),
            pltpu.VMEM((padded, channels), bf16),
            pltpu.VMEM((padded, 3 * channels), bf16),
            pltpu.SemaphoreType.DMA((5,)),
            pltpu.SemaphoreType.DMA((owners,)),
            pltpu.SemaphoreType.DMA((owners,)),
            pltpu.SemaphoreType.DMA((owners,)),
            pltpu.SemaphoreType.DMA((owners,)),
            pltpu.SemaphoreType.DMA((2, 2)),
            pltpu.SemaphoreType.DMA((2, 2)),
        ],
        compiler_params=pltpu.CompilerParams(
            collective_id=0, has_side_effects=True, vmem_limit_bytes=56 * 2**20
        ),
    )(
        features.reshape(tokens_dev, model_width),
        codes.T,
        codes,
        gates.reshape(tokens_dev, 2),
        w_in,
        w_out,
        w_proj,
        kernel_one.reshape(3, 3 * channels, channels),
        kernel_two.reshape(3, 3 * channels, channels),
    )
    return joined.reshape(maps_dev, rows_dev, width_cols, channels)


def solution(mesh):
    placed = (
        P("expert", "slab", None, None),
        P("expert", "slab", None, None),
        P("expert", "slab", None, None),
        P("expert", "slab", None, None),
        P("expert", None, None),
        P("expert", None, None),
        P(),
        P(),
        P(),
    )
    return jax.shard_map(
        functools.partial(shards, mesh.shape["expert"], mesh.shape["slab"]),
        mesh=mesh,
        in_specs=placed,
        out_specs=P("expert", "slab", None, None),
        check_vma=False,
    )
```

```python
import functools

import jax
import jax.numpy as jnp
from jax import lax
from jax.experimental import pallas as pl
from jax.experimental.pallas import tpu as pltpu
from jax.sharding import PartitionSpec as P

MESH = pl.DeviceIdType.MESH
HIDDEN_TILE = 1024
FUSE_TILE = 512


def gelu(value):
    inner = 0.7978845608028654 * (value + 0.044715 * (value * value * value))
    half = 0.5 * value
    return half + half * jnp.tanh(inner)


def paired(me, step, count):
    partner, bit = 0, 1
    while bit < count:
        partner = partner + ((me // bit + step // bit) % 2) * bit
        bit *= 2
    return partner


def kernel(
    owners, slabs, capacity, rows, cols,
    features, codes_row, codes_col, gates, w_in_hbm, w_out_hbm, w_proj_hbm, one_hbm, two_hbm,
    joined,
    w_in, w_out, w_proj, one, two, fused, normed, sent, held, back, returned, total,
    neck, hidden, columns,
    load_sem, sent_sem, held_sem, back_sem, returned_sem, edge_sent, edge_held,
):
    me = lax.axis_index("expert")
    slab = lax.axis_index("slab")
    tokens, width = features.shape
    hidden_units = w_in.shape[1]
    loads = [
        pltpu.make_async_copy(source, target, load_sem.at[place])
        for place, (source, target) in enumerate(
            [(w_out_hbm.at[0], w_out), (w_proj_hbm, w_proj), (w_in_hbm.at[0], w_in),
             (one_hbm, one), (two_hbm, two)]
        )
    ]
    for load in loads:
        load.start()

    barrier = pltpu.get_barrier_semaphore()

    @pl.loop(1, owners)
    def _(step):
        pl.semaphore_signal(
            barrier, inc=1, device_id=(slab, paired(me, step, owners)), device_id_type=MESH
        )

    @pl.when(slab > 0)
    def _():
        pl.semaphore_signal(barrier, inc=1, device_id=(slab - 1, me), device_id_type=MESH)

    @pl.when(slab < slabs - 1)
    def _():
        pl.semaphore_signal(barrier, inc=1, device_id=(slab + 1, me), device_id_type=MESH)

    @pl.loop(0, tokens // cols)
    def _(chunk):
        piece = pl.ds(pl.multiple_of(chunk * cols, cols), cols)
        wide = features[piece, :].astype(jnp.float32)
        scale = lax.rsqrt(jnp.mean(wide * wide, axis=1, keepdims=True) + 1e-06)
        normed[piece, :] = (wide * scale).astype(jnp.bfloat16)

    neighbours = jnp.minimum(slab, 1) + jnp.minimum(slabs - 1 - slab, 1)
    pl.semaphore_wait(barrier, owners - 1 + neighbours)

    def dispatch(step):
        return pltpu.make_async_remote_copy(
            src_ref=sent.at[step], dst_ref=held.at[step],
            send_sem=sent_sem.at[step], recv_sem=held_sem.at[step],
            device_id=(slab, paired(me, step, owners)), device_id_type=MESH,
        )

    def giveback(step):
        return pltpu.make_async_remote_copy(
            src_ref=back.at[step], dst_ref=returned.at[step],
            send_sem=back_sem.at[step], recv_sem=returned_sem.at[step],
            device_id=(slab, paired(me, step, owners)), device_id_type=MESH,
        )

    def packed(step):
        slot = paired(me, step, owners) * capacity + lax.broadcasted_iota(
            jnp.int32, (capacity, tokens), 0
        )
        chosen = (codes_row[0:1, :] == slot) | (codes_row[1:2, :] == slot)
        choice = jnp.where(chosen, 1.0, 0.0).astype(jnp.bfloat16)
        return jnp.dot(choice, normed[...], preferred_element_type=jnp.float32).astype(jnp.bfloat16)

    @pl.loop(0, owners - 1)
    def _(turn):
        step = owners - 1 - turn
        sent[step] = packed(step)
        dispatch(step).start()

    held[0] = packed(0)

    loads[0].wait()
    loads[1].wait()

    @pl.loop(0, hidden_units // FUSE_TILE)
    def _(tile):
        piece = pl.ds(pl.multiple_of(tile * FUSE_TILE, FUSE_TILE), FUSE_TILE)
        fused[piece, :] = jnp.dot(
            w_out[piece, :], w_proj[...], preferred_element_type=jnp.float32
        ).astype(jnp.bfloat16)

    total[0:tokens, :] = jnp.dot(features[...], w_proj[...], preferred_element_type=jnp.float32)
    loads[2].wait()

    def expert(step):
        block = held[step]
        result = jnp.zeros((capacity, fused.shape[1]), jnp.float32)
        for tile in range(hidden_units // HIDDEN_TILE):
            piece = slice(tile * HIDDEN_TILE, (tile + 1) * HIDDEN_TILE)
            pre = jnp.dot(block, w_in[:, piece], preferred_element_type=jnp.float32)
            result = result + jnp.dot(
                gelu(pre).astype(jnp.bfloat16), fused[piece, :], preferred_element_type=jnp.float32
            )
        back[step] = result.astype(jnp.bfloat16)

    def combine(step, source):
        slot = paired(me, step, owners) * capacity + lax.broadcasted_iota(
            jnp.int32, (tokens, capacity), 1
        )
        outcome = source[step]
        for choice in range(2):
            chosen = codes_col[:, choice : choice + 1] == slot
            picked = jnp.dot(
                jnp.where(chosen, 1.0, 0.0).astype(jnp.bfloat16), outcome,
                preferred_element_type=jnp.float32,
            )
            total[0:tokens, :] += gates[:, choice : choice + 1] * picked

    def serve(step):
        dispatch(step).wait_recv()
        expert(step)
        giveback(step).start()

    def gather(step):
        giveback(step).wait_recv()
        combine(step, returned)

    near = owners // 2
    expert(0)

    @pl.loop(1, near)
    def _(step):
        serve(step)

    combine(0, back)

    @pl.loop(1, near)
    def _(step):
        gather(step)

    @pl.loop(0, owners - near)
    def _(turn):
        serve(owners - 1 - turn)

    @pl.loop(0, owners - near)
    def _(turn):
        gather(owners - 1 - turn)

    loads[3].wait()
    loads[4].wait()
    halo = 2 * cols
    end = halo + tokens
    inside = slice(halo, end)
    up = pltpu.make_async_remote_copy(
        src_ref=neck.at[pl.ds(halo, halo)], dst_ref=neck.at[pl.ds(end, halo)],
        send_sem=edge_sent.at[0], recv_sem=edge_held.at[0],
        device_id=(jnp.maximum(slab - 1, 0), me), device_id_type=MESH,
    )
    down = pltpu.make_async_remote_copy(
        src_ref=neck.at[pl.ds(tokens, halo)], dst_ref=neck.at[pl.ds(0, halo)],
        send_sem=edge_sent.at[1], recv_sem=edge_held.at[1],
        device_id=(jnp.minimum(slab + 1, slabs - 1), me), device_id_type=MESH,
    )

    def spread(field, start, count):
        piece = slice(start, start + count)
        centre = field[piece, :]
        channels = centre.shape[1]
        wide = centre.astype(jnp.float32)
        column = lax.broadcasted_iota(jnp.int32, (count, 1), 0) % cols
        columns[piece, 0:channels] = jnp.where(
            column == 0, 0.0, pltpu.roll(wide, 1, 0)
        ).astype(jnp.bfloat16)
        columns[piece, channels : 2 * channels] = centre
        columns[piece, 2 * channels : 3 * channels] = jnp.where(
            column == cols - 1, 0.0, pltpu.roll(wide, count - 1, 0)
        ).astype(jnp.bfloat16)

    def tapped(taps, row, start, count):
        return jnp.dot(
            columns[start : start + count, :], taps[row], preferred_element_type=jnp.float32
        )

    neck[inside, :] = total[0:tokens, :].astype(jnp.bfloat16)

    @pl.when(slab > 0)
    def _():
        up.start()

    @pl.when(slab < slabs - 1)
    def _():
        down.start()

    @pl.when(slab == 0)
    def _():
        neck[0:halo, :] = jnp.zeros((halo, neck.shape[1]), jnp.bfloat16)

    @pl.when(slab == slabs - 1)
    def _():
        neck[end : end + halo, :] = jnp.zeros((halo, neck.shape[1]), jnp.bfloat16)

    spread(neck, halo, tokens)
    total[0:tokens, :] = tapped(one, 2, halo, tokens)
    total[tokens:end, :] = jnp.zeros((halo, total.shape[1]), jnp.float32)
    total[cols : cols + tokens, :] += tapped(one, 1, halo, tokens)
    total[halo:end, :] += tapped(one, 0, halo, tokens)

    @pl.when(slab > 0)
    def _():
        down.wait_recv()

    @pl.when(slab < slabs - 1)
    def _():
        up.wait_recv()

    spread(neck, 0, halo)
    spread(neck, end, halo)
    total[0:halo, :] += tapped(one, 0, 0, halo)
    total[0:cols, :] += tapped(one, 1, cols, cols)
    total[tokens:end, :] += tapped(one, 2, end, halo)
    total[end - cols : end, :] += tapped(one, 1, end, cols)
    hidden[...] = gelu(total[...]).astype(jnp.bfloat16)

    @pl.when(slab == 0)
    def _():
        hidden[0:cols, :] = jnp.zeros((cols, hidden.shape[1]), jnp.bfloat16)

    @pl.when(slab == slabs - 1)
    def _():
        hidden[end - cols : end, :] = jnp.zeros((cols, hidden.shape[1]), jnp.bfloat16)

    spread(hidden, 0, end)
    joined[...] = (
        neck[inside, :].astype(jnp.float32)
        + tapped(two, 0, 0, tokens)
        + tapped(two, 1, cols, tokens)
        + tapped(two, 2, halo, tokens)
    ).astype(jnp.bfloat16)

    @pl.loop(1, owners)
    def _(step):
        dispatch(step).wait_send()
        giveback(step).wait_send()

    @pl.when(slab > 0)
    def _():
        up.wait_send()

    @pl.when(slab < slabs - 1)
    def _():
        down.wait_send()


def shards(owners, slabs, features, expert_ids, positions, gates, w_in, w_out, w_proj, kernel_one,
           kernel_two):
    maps_dev, rows_dev, width_cols, model_width = features.shape
    tokens_dev = maps_dev * rows_dev * width_cols
    local_experts, _, hidden_units = w_in.shape
    capacity = 3 * tokens_dev // (owners * local_experts)
    channels = w_proj.shape[1]
    codes = jnp.where(positions < capacity, expert_ids * capacity + positions, -1)
    codes = codes.reshape(tokens_dev, 2)
    vmem = pl.BlockSpec(memory_space=pltpu.VMEM)
    anywhere = pl.BlockSpec(memory_space=pl.ANY)
    bf16, f32 = jnp.bfloat16, jnp.float32
    padded = tokens_dev + 2 * width_cols
    joined = pl.pallas_call(
        functools.partial(kernel, owners, slabs, capacity, rows_dev, width_cols),
        out_shape=jax.ShapeDtypeStruct((tokens_dev, channels), bf16),
        in_specs=[vmem] * 4 + [anywhere] * 5,
        out_specs=vmem,
        scratch_shapes=[
            pltpu.VMEM((model_width, hidden_units), bf16),
            pltpu.VMEM((hidden_units, model_width), bf16),
            pltpu.VMEM((model_width, channels), bf16),
            pltpu.VMEM((3, 3 * channels, channels), bf16),
            pltpu.VMEM((3, 3 * channels, channels), bf16),
            pltpu.VMEM((hidden_units, channels), bf16),
            pltpu.VMEM((tokens_dev, model_width), bf16),
            pltpu.VMEM((owners, capacity, model_width), bf16),
            pltpu.VMEM((owners, capacity, model_width), bf16),
            pltpu.VMEM((owners, capacity, channels), bf16),
            pltpu.VMEM((owners, capacity, channels), bf16),
            pltpu.VMEM((padded, channels), f32),
            pltpu.VMEM((padded + 2 * width_cols, channels), bf16),
            pltpu.VMEM((padded, channels), bf16),
            pltpu.VMEM((padded + 2 * width_cols, 3 * channels), bf16),
            pltpu.SemaphoreType.DMA((5,)),
            pltpu.SemaphoreType.DMA((owners,)),
            pltpu.SemaphoreType.DMA((owners,)),
            pltpu.SemaphoreType.DMA((owners,)),
            pltpu.SemaphoreType.DMA((owners,)),
            pltpu.SemaphoreType.DMA((2,)),
            pltpu.SemaphoreType.DMA((2,)),
        ],
        compiler_params=pltpu.CompilerParams(
            collective_id=0, has_side_effects=True, vmem_limit_bytes=56 * 2**20
        ),
    )(
        features.reshape(tokens_dev, model_width),
        codes.T,
        codes,
        gates.reshape(tokens_dev, 2),
        w_in,
        w_out,
        w_proj,
        kernel_one.reshape(3, 3 * channels, channels),
        kernel_two.reshape(3, 3 * channels, channels),
    )
    return joined.reshape(maps_dev, rows_dev, width_cols, channels)


def solution(mesh):
    placed = (
        P("expert", "slab", None, None),
        P("expert", "slab", None, None),
        P("expert", "slab", None, None),
        P("expert", "slab", None, None),
        P("expert", None, None),
        P("expert", None, None),
        P(),
        P(),
        P(),
    )
    return jax.shard_map(
        functools.partial(shards, mesh.shape["expert"], mesh.shape["slab"]),
        mesh=mesh,
        in_specs=placed,
        out_specs=P("expert", "slab", None, None),
        check_vma=False,
    )
```

```python
import functools

import jax
import jax.numpy as jnp
from jax import lax
from jax.experimental import pallas as pl
from jax.experimental.pallas import tpu as pltpu
from jax.sharding import PartitionSpec as P

MESH = pl.DeviceIdType.MESH
HIDDEN_TILE = 1024
FUSE_TILE = 512


def gelu(value):
    inner = 0.7978845608028654 * (value + 0.044715 * (value * value * value))
    half = 0.5 * value
    return half + half * jnp.tanh(inner)


def paired(me, step, count):
    partner, bit = 0, 1
    while bit < count:
        partner = partner + ((me // bit + step // bit) % 2) * bit
        bit *= 2
    return partner


def kernel(
    owners, slabs, capacity, rows, cols,
    features, codes_row, gates, w_in_hbm, w_out_hbm, w_proj_hbm, one_hbm, two_hbm,
    joined,
    w_in, w_out, w_proj, one, two, fused, normed, sent, held, back, returned, total,
    neck, hidden, columns,
    load_sem, sent_sem, held_sem, back_sem, returned_sem, edge_sent, edge_held,
):
    me = lax.axis_index("expert")
    slab = lax.axis_index("slab")
    tokens, width = features.shape
    hidden_units = w_in.shape[1]
    loads = [
        pltpu.make_async_copy(source, target, load_sem.at[place])
        for place, (source, target) in enumerate(
            [(w_out_hbm.at[0], w_out), (w_proj_hbm, w_proj), (w_in_hbm.at[0], w_in),
             (one_hbm, one), (two_hbm, two)]
        )
    ]
    for load in loads:
        load.start()

    barrier = pltpu.get_barrier_semaphore()

    @pl.loop(1, owners)
    def _(step):
        pl.semaphore_signal(
            barrier, inc=1, device_id=(slab, paired(me, step, owners)), device_id_type=MESH
        )

    @pl.when(slab > 0)
    def _():
        pl.semaphore_signal(barrier, inc=1, device_id=(slab - 1, me), device_id_type=MESH)

    @pl.when(slab < slabs - 1)
    def _():
        pl.semaphore_signal(barrier, inc=1, device_id=(slab + 1, me), device_id_type=MESH)

    @pl.loop(0, tokens // cols)
    def _(chunk):
        piece = pl.ds(pl.multiple_of(chunk * cols, cols), cols)
        wide = features[piece, :].astype(jnp.float32)
        scale = lax.rsqrt(jnp.mean(wide * wide, axis=1, keepdims=True) + 1e-06)
        normed[piece, :] = (wide * scale).astype(jnp.bfloat16)

    neighbours = jnp.minimum(slab, 1) + jnp.minimum(slabs - 1 - slab, 1)
    pl.semaphore_wait(barrier, owners - 1 + neighbours)

    def dispatch(step):
        return pltpu.make_async_remote_copy(
            src_ref=sent.at[step], dst_ref=held.at[step],
            send_sem=sent_sem.at[step], recv_sem=held_sem.at[step],
            device_id=(slab, paired(me, step, owners)), device_id_type=MESH,
        )

    def giveback(step):
        return pltpu.make_async_remote_copy(
            src_ref=back.at[step], dst_ref=returned.at[step],
            send_sem=back_sem.at[step], recv_sem=returned_sem.at[step],
            device_id=(slab, paired(me, step, owners)), device_id_type=MESH,
        )

    def packed(step):
        slot = paired(me, step, owners) * capacity + lax.broadcasted_iota(
            jnp.int32, (capacity, tokens), 0
        )
        chosen = (codes_row[0:1, :] == slot) | (codes_row[1:2, :] == slot)
        choice = jnp.where(chosen, 1.0, 0.0).astype(jnp.bfloat16)
        return jnp.dot(choice, normed[...], preferred_element_type=jnp.float32).astype(jnp.bfloat16)

    @pl.loop(0, owners - 1)
    def _(turn):
        step = owners - 1 - turn
        sent[step] = packed(step)
        dispatch(step).start()

    held[0] = packed(0)

    loads[0].wait()
    loads[1].wait()

    @pl.loop(0, hidden_units // FUSE_TILE)
    def _(tile):
        piece = pl.ds(pl.multiple_of(tile * FUSE_TILE, FUSE_TILE), FUSE_TILE)
        fused[piece, :] = jnp.dot(
            w_out[piece, :], w_proj[...], preferred_element_type=jnp.float32
        ).astype(jnp.bfloat16)

    total[0:tokens, :] = jnp.dot(features[...], w_proj[...], preferred_element_type=jnp.float32)
    loads[2].wait()

    def expert(step):
        block = held[step]
        result = jnp.zeros((capacity, fused.shape[1]), jnp.float32)
        for tile in range(hidden_units // HIDDEN_TILE):
            piece = slice(tile * HIDDEN_TILE, (tile + 1) * HIDDEN_TILE)
            pre = jnp.dot(block, w_in[:, piece], preferred_element_type=jnp.float32)
            result = result + jnp.dot(
                gelu(pre).astype(jnp.bfloat16), fused[piece, :], preferred_element_type=jnp.float32
            )
        back[step] = result.astype(jnp.bfloat16)

    def combine(step, source):
        slot = paired(me, step, owners) * capacity + lax.broadcasted_iota(
            jnp.int32, (capacity, tokens), 0
        )
        weight = jnp.where(codes_row[0:1, :] == slot, gates[0:1, :], 0.0) + jnp.where(
            codes_row[1:2, :] == slot, gates[1:2, :], 0.0
        )
        coarse = weight.astype(jnp.bfloat16)
        fine = (weight - coarse.astype(jnp.float32)).astype(jnp.bfloat16)
        outcome = source[step]
        for part in (coarse, fine):
            total[0:tokens, :] += lax.dot_general(
                part, outcome, (((0,), (0,)), ((), ())), preferred_element_type=jnp.float32
            )

    def serve(step):
        dispatch(step).wait_recv()
        expert(step)
        giveback(step).start()

    def gather(step):
        giveback(step).wait_recv()
        combine(step, returned)

    near = owners // 2
    expert(0)

    @pl.loop(1, near)
    def _(step):
        serve(step)

    combine(0, back)

    @pl.loop(1, near)
    def _(step):
        gather(step)

    @pl.loop(0, owners - near)
    def _(turn):
        serve(owners - 1 - turn)

    @pl.loop(0, owners - near)
    def _(turn):
        gather(owners - 1 - turn)

    loads[3].wait()
    loads[4].wait()
    halo = 2 * cols
    end = halo + tokens
    inside = slice(halo, end)
    up = pltpu.make_async_remote_copy(
        src_ref=neck.at[pl.ds(halo, halo)], dst_ref=neck.at[pl.ds(end, halo)],
        send_sem=edge_sent.at[0], recv_sem=edge_held.at[0],
        device_id=(jnp.maximum(slab - 1, 0), me), device_id_type=MESH,
    )
    down = pltpu.make_async_remote_copy(
        src_ref=neck.at[pl.ds(tokens, halo)], dst_ref=neck.at[pl.ds(0, halo)],
        send_sem=edge_sent.at[1], recv_sem=edge_held.at[1],
        device_id=(jnp.minimum(slab + 1, slabs - 1), me), device_id_type=MESH,
    )

    def spread(field, start, count):
        piece = slice(start, start + count)
        centre = field[piece, :]
        channels = centre.shape[1]
        wide = centre.astype(jnp.float32)
        column = lax.broadcasted_iota(jnp.int32, (count, 1), 0) % cols
        columns[piece, 0:channels] = jnp.where(
            column == 0, 0.0, pltpu.roll(wide, 1, 0)
        ).astype(jnp.bfloat16)
        columns[piece, channels : 2 * channels] = centre
        columns[piece, 2 * channels : 3 * channels] = jnp.where(
            column == cols - 1, 0.0, pltpu.roll(wide, count - 1, 0)
        ).astype(jnp.bfloat16)

    def tapped(taps, row, start, count):
        return jnp.dot(
            columns[start : start + count, :], taps[row], preferred_element_type=jnp.float32
        )

    neck[inside, :] = total[0:tokens, :].astype(jnp.bfloat16)

    @pl.when(slab > 0)
    def _():
        up.start()

    @pl.when(slab < slabs - 1)
    def _():
        down.start()

    @pl.when(slab == 0)
    def _():
        neck[0:halo, :] = jnp.zeros((halo, neck.shape[1]), jnp.bfloat16)

    @pl.when(slab == slabs - 1)
    def _():
        neck[end : end + halo, :] = jnp.zeros((halo, neck.shape[1]), jnp.bfloat16)

    spread(neck, halo, tokens)
    total[0:tokens, :] = tapped(one, 2, halo, tokens)
    total[tokens:end, :] = jnp.zeros((halo, total.shape[1]), jnp.float32)
    total[cols : cols + tokens, :] += tapped(one, 1, halo, tokens)
    total[halo:end, :] += tapped(one, 0, halo, tokens)

    @pl.when(slab > 0)
    def _():
        down.wait_recv()

    @pl.when(slab < slabs - 1)
    def _():
        up.wait_recv()

    spread(neck, 0, halo)
    spread(neck, end, halo)
    total[0:halo, :] += tapped(one, 0, 0, halo)
    total[0:cols, :] += tapped(one, 1, cols, cols)
    total[tokens:end, :] += tapped(one, 2, end, halo)
    total[end - cols : end, :] += tapped(one, 1, end, cols)
    hidden[...] = gelu(total[...]).astype(jnp.bfloat16)

    @pl.when(slab == 0)
    def _():
        hidden[0:cols, :] = jnp.zeros((cols, hidden.shape[1]), jnp.bfloat16)

    @pl.when(slab == slabs - 1)
    def _():
        hidden[end - cols : end, :] = jnp.zeros((cols, hidden.shape[1]), jnp.bfloat16)

    spread(hidden, 0, end)
    joined[...] = (
        neck[inside, :].astype(jnp.float32)
        + tapped(two, 0, 0, tokens)
        + tapped(two, 1, cols, tokens)
        + tapped(two, 2, halo, tokens)
    ).astype(jnp.bfloat16)

    @pl.loop(1, owners)
    def _(step):
        dispatch(step).wait_send()
        giveback(step).wait_send()

    @pl.when(slab > 0)
    def _():
        up.wait_send()

    @pl.when(slab < slabs - 1)
    def _():
        down.wait_send()


def shards(owners, slabs, features, expert_ids, positions, gates, w_in, w_out, w_proj, kernel_one,
           kernel_two):
    maps_dev, rows_dev, width_cols, model_width = features.shape
    tokens_dev = maps_dev * rows_dev * width_cols
    local_experts, _, hidden_units = w_in.shape
    capacity = 3 * tokens_dev // (owners * local_experts)
    channels = w_proj.shape[1]
    codes = jnp.where(positions < capacity, expert_ids * capacity + positions, -1)
    codes = codes.reshape(tokens_dev, 2).T
    vmem = pl.BlockSpec(memory_space=pltpu.VMEM)
    anywhere = pl.BlockSpec(memory_space=pl.ANY)
    bf16, f32 = jnp.bfloat16, jnp.float32
    padded = tokens_dev + 2 * width_cols
    joined = pl.pallas_call(
        functools.partial(kernel, owners, slabs, capacity, rows_dev, width_cols),
        out_shape=jax.ShapeDtypeStruct((tokens_dev, channels), bf16),
        in_specs=[vmem] * 3 + [anywhere] * 5,
        out_specs=vmem,
        scratch_shapes=[
            pltpu.VMEM((model_width, hidden_units), bf16),
            pltpu.VMEM((hidden_units, model_width), bf16),
            pltpu.VMEM((model_width, channels), bf16),
            pltpu.VMEM((3, 3 * channels, channels), bf16),
            pltpu.VMEM((3, 3 * channels, channels), bf16),
            pltpu.VMEM((hidden_units, channels), bf16),
            pltpu.VMEM((tokens_dev, model_width), bf16),
            pltpu.VMEM((owners, capacity, model_width), bf16),
            pltpu.VMEM((owners, capacity, model_width), bf16),
            pltpu.VMEM((owners, capacity, channels), bf16),
            pltpu.VMEM((owners, capacity, channels), bf16),
            pltpu.VMEM((padded, channels), f32),
            pltpu.VMEM((padded + 2 * width_cols, channels), bf16),
            pltpu.VMEM((padded, channels), bf16),
            pltpu.VMEM((padded + 2 * width_cols, 3 * channels), bf16),
            pltpu.SemaphoreType.DMA((5,)),
            pltpu.SemaphoreType.DMA((owners,)),
            pltpu.SemaphoreType.DMA((owners,)),
            pltpu.SemaphoreType.DMA((owners,)),
            pltpu.SemaphoreType.DMA((owners,)),
            pltpu.SemaphoreType.DMA((2,)),
            pltpu.SemaphoreType.DMA((2,)),
        ],
        compiler_params=pltpu.CompilerParams(
            collective_id=0, has_side_effects=True, vmem_limit_bytes=56 * 2**20
        ),
    )(
        features.reshape(tokens_dev, model_width),
        codes,
        gates.reshape(tokens_dev, 2).T,
        w_in,
        w_out,
        w_proj,
        kernel_one.reshape(3, 3 * channels, channels),
        kernel_two.reshape(3, 3 * channels, channels),
    )
    return joined.reshape(maps_dev, rows_dev, width_cols, channels)


def solution(mesh):
    placed = (
        P("expert", "slab", None, None),
        P("expert", "slab", None, None),
        P("expert", "slab", None, None),
        P("expert", "slab", None, None),
        P("expert", None, None),
        P("expert", None, None),
        P(),
        P(),
        P(),
    )
    return jax.shard_map(
        functools.partial(shards, mesh.shape["expert"], mesh.shape["slab"]),
        mesh=mesh,
        in_specs=placed,
        out_specs=P("expert", "slab", None, None),
        check_vma=False,
    )
```

```python
import functools

import jax
import jax.numpy as jnp
from jax import lax
from jax.experimental import pallas as pl
from jax.experimental.pallas import tpu as pltpu
from jax.sharding import PartitionSpec as P

MESH = pl.DeviceIdType.MESH
HIDDEN_TILE = 1024
FUSE_TILE = 512


def gelu(value):
    inner = 0.7978845608028654 * (value + 0.044715 * (value * value * value))
    half = 0.5 * value
    return half + half * jnp.tanh(inner)


def paired(me, step, count):
    partner, bit = 0, 1
    while bit < count:
        partner = partner + ((me // bit + step // bit) % 2) * bit
        bit *= 2
    return partner


def kernel(
    owners, slabs, capacity, rows, cols,
    features, codes_row, gates, w_in_hbm, w_out_hbm, w_proj_hbm, one_hbm, two_hbm,
    joined,
    w_in, w_out, w_proj, one, two, fused, normed, sent, held, back, returned, total,
    neck, hidden, columns,
    load_sem, sent_sem, held_sem, back_sem, returned_sem, edge_sent, edge_held,
):
    me = lax.axis_index("expert")
    slab = lax.axis_index("slab")
    tokens, width = features.shape
    hidden_units = w_in.shape[1]
    loads = [
        pltpu.make_async_copy(source, target, load_sem.at[place])
        for place, (source, target) in enumerate(
            [(w_out_hbm.at[0], w_out), (w_proj_hbm, w_proj), (w_in_hbm.at[0], w_in),
             (one_hbm, one), (two_hbm, two)]
        )
    ]
    for load in loads:
        load.start()

    barrier = pltpu.get_barrier_semaphore()

    @pl.loop(1, owners)
    def _(step):
        pl.semaphore_signal(
            barrier, inc=1, device_id=(slab, paired(me, step, owners)), device_id_type=MESH
        )

    @pl.when(slab > 0)
    def _():
        pl.semaphore_signal(barrier, inc=1, device_id=(slab - 1, me), device_id_type=MESH)

    @pl.when(slab < slabs - 1)
    def _():
        pl.semaphore_signal(barrier, inc=1, device_id=(slab + 1, me), device_id_type=MESH)

    @pl.loop(0, tokens // cols)
    def _(chunk):
        piece = pl.ds(pl.multiple_of(chunk * cols, cols), cols)
        wide = features[piece, :].astype(jnp.float32)
        scale = lax.rsqrt(jnp.mean(wide * wide, axis=1, keepdims=True) + 1e-06)
        normed[piece, :] = (wide * scale).astype(jnp.bfloat16)

    neighbours = jnp.minimum(slab, 1) + jnp.minimum(slabs - 1 - slab, 1)
    pl.semaphore_wait(barrier, owners - 1 + neighbours)

    def dispatch(step):
        return pltpu.make_async_remote_copy(
            src_ref=sent.at[step], dst_ref=held.at[step],
            send_sem=sent_sem.at[step], recv_sem=held_sem.at[step],
            device_id=(slab, paired(me, step, owners)), device_id_type=MESH,
        )

    def giveback(step):
        return pltpu.make_async_remote_copy(
            src_ref=back.at[step], dst_ref=returned.at[step],
            send_sem=back_sem.at[step], recv_sem=returned_sem.at[step],
            device_id=(slab, paired(me, step, owners)), device_id_type=MESH,
        )

    def packed(step):
        slot = paired(me, step, owners) * capacity + lax.broadcasted_iota(
            jnp.int32, (capacity, tokens), 0
        )
        chosen = (codes_row[0:1, :] == slot) | (codes_row[1:2, :] == slot)
        choice = jnp.where(chosen, 1.0, 0.0).astype(jnp.bfloat16)
        return jnp.dot(choice, normed[...], preferred_element_type=jnp.float32).astype(jnp.bfloat16)

    @pl.loop(0, owners - 1)
    def _(turn):
        step = owners - 1 - turn
        sent[step] = packed(step)
        dispatch(step).start()

    held[0] = packed(0)

    loads[0].wait()
    loads[1].wait()

    @pl.loop(0, hidden_units // FUSE_TILE)
    def _(tile):
        piece = pl.ds(pl.multiple_of(tile * FUSE_TILE, FUSE_TILE), FUSE_TILE)
        fused[piece, :] = jnp.dot(
            w_out[piece, :], w_proj[...], preferred_element_type=jnp.float32
        ).astype(jnp.bfloat16)

    total[0:tokens, :] = jnp.dot(features[...], w_proj[...], preferred_element_type=jnp.float32)
    loads[2].wait()

    def expert(step):
        block = held[step]
        result = jnp.zeros((capacity, fused.shape[1]), jnp.float32)
        for tile in range(hidden_units // HIDDEN_TILE):
            piece = slice(tile * HIDDEN_TILE, (tile + 1) * HIDDEN_TILE)
            pre = jnp.dot(block, w_in[:, piece], preferred_element_type=jnp.float32)
            result = result + jnp.dot(
                gelu(pre).astype(jnp.bfloat16), fused[piece, :], preferred_element_type=jnp.float32
            )
        back[step] = result.astype(jnp.bfloat16)

    def combine(step, source):
        slot = paired(me, step, owners) * capacity + lax.broadcasted_iota(
            jnp.int32, (capacity, tokens), 0
        )
        weight = jnp.where(codes_row[0:1, :] == slot, gates[0:1, :], 0.0) + jnp.where(
            codes_row[1:2, :] == slot, gates[1:2, :], 0.0
        )
        coarse = weight.astype(jnp.bfloat16)
        fine = (weight - coarse.astype(jnp.float32)).astype(jnp.bfloat16)
        outcome = source[step]
        for part in (coarse, fine):
            total[0:tokens, :] += lax.dot_general(
                part, outcome, (((0,), (0,)), ((), ())), preferred_element_type=jnp.float32
            )

    def serve(step):
        dispatch(step).wait_recv()
        expert(step)
        giveback(step).start()

    def gather(step):
        giveback(step).wait_recv()
        combine(step, returned)

    expert(0)
    combine(0, back)

    @pl.loop(0, owners - 1)
    def _(turn):
        serve(owners - 1 - turn)

    @pl.loop(0, owners - 1)
    def _(turn):
        gather(owners - 1 - turn)

    loads[3].wait()
    loads[4].wait()
    halo = 2 * cols
    end = halo + tokens
    inside = slice(halo, end)
    up = pltpu.make_async_remote_copy(
        src_ref=neck.at[pl.ds(halo, halo)], dst_ref=neck.at[pl.ds(end, halo)],
        send_sem=edge_sent.at[0], recv_sem=edge_held.at[0],
        device_id=(jnp.maximum(slab - 1, 0), me), device_id_type=MESH,
    )
    down = pltpu.make_async_remote_copy(
        src_ref=neck.at[pl.ds(tokens, halo)], dst_ref=neck.at[pl.ds(0, halo)],
        send_sem=edge_sent.at[1], recv_sem=edge_held.at[1],
        device_id=(jnp.minimum(slab + 1, slabs - 1), me), device_id_type=MESH,
    )

    def spread(field, start, count):
        piece = slice(start, start + count)
        centre = field[piece, :]
        channels = centre.shape[1]
        wide = centre.astype(jnp.float32)
        column = lax.broadcasted_iota(jnp.int32, (count, 1), 0) % cols
        columns[piece, 0:channels] = jnp.where(
            column == 0, 0.0, pltpu.roll(wide, 1, 0)
        ).astype(jnp.bfloat16)
        columns[piece, channels : 2 * channels] = centre
        columns[piece, 2 * channels : 3 * channels] = jnp.where(
            column == cols - 1, 0.0, pltpu.roll(wide, count - 1, 0)
        ).astype(jnp.bfloat16)

    def tapped(taps, row, start, count):
        return jnp.dot(
            columns[start : start + count, :], taps[row], preferred_element_type=jnp.float32
        )

    neck[inside, :] = total[0:tokens, :].astype(jnp.bfloat16)

    @pl.when(slab > 0)
    def _():
        up.start()

    @pl.when(slab < slabs - 1)
    def _():
        down.start()

    @pl.when(slab == 0)
    def _():
        neck[0:halo, :] = jnp.zeros((halo, neck.shape[1]), jnp.bfloat16)

    @pl.when(slab == slabs - 1)
    def _():
        neck[end : end + halo, :] = jnp.zeros((halo, neck.shape[1]), jnp.bfloat16)

    spread(neck, halo, tokens)
    total[0:tokens, :] = tapped(one, 2, halo, tokens)
    total[tokens:end, :] = jnp.zeros((halo, total.shape[1]), jnp.float32)
    total[cols : cols + tokens, :] += tapped(one, 1, halo, tokens)
    total[halo:end, :] += tapped(one, 0, halo, tokens)

    @pl.when(slab > 0)
    def _():
        down.wait_recv()

    @pl.when(slab < slabs - 1)
    def _():
        up.wait_recv()

    spread(neck, 0, halo)
    spread(neck, end, halo)
    total[0:halo, :] += tapped(one, 0, 0, halo)
    total[0:cols, :] += tapped(one, 1, cols, cols)
    total[tokens:end, :] += tapped(one, 2, end, halo)
    total[end - cols : end, :] += tapped(one, 1, end, cols)
    hidden[...] = gelu(total[...]).astype(jnp.bfloat16)

    @pl.when(slab == 0)
    def _():
        hidden[0:cols, :] = jnp.zeros((cols, hidden.shape[1]), jnp.bfloat16)

    @pl.when(slab == slabs - 1)
    def _():
        hidden[end - cols : end, :] = jnp.zeros((cols, hidden.shape[1]), jnp.bfloat16)

    spread(hidden, 0, end)
    joined[...] = (
        neck[inside, :].astype(jnp.float32)
        + tapped(two, 0, 0, tokens)
        + tapped(two, 1, cols, tokens)
        + tapped(two, 2, halo, tokens)
    ).astype(jnp.bfloat16)

    @pl.loop(1, owners)
    def _(step):
        dispatch(step).wait_send()
        giveback(step).wait_send()

    @pl.when(slab > 0)
    def _():
        up.wait_send()

    @pl.when(slab < slabs - 1)
    def _():
        down.wait_send()


def shards(owners, slabs, features, expert_ids, positions, gates, w_in, w_out, w_proj, kernel_one,
           kernel_two):
    maps_dev, rows_dev, width_cols, model_width = features.shape
    tokens_dev = maps_dev * rows_dev * width_cols
    local_experts, _, hidden_units = w_in.shape
    capacity = 3 * tokens_dev // (owners * local_experts)
    channels = w_proj.shape[1]
    codes = jnp.where(positions < capacity, expert_ids * capacity + positions, -1)
    codes = codes.reshape(tokens_dev, 2).T
    vmem = pl.BlockSpec(memory_space=pltpu.VMEM)
    anywhere = pl.BlockSpec(memory_space=pl.ANY)
    bf16, f32 = jnp.bfloat16, jnp.float32
    padded = tokens_dev + 2 * width_cols
    joined = pl.pallas_call(
        functools.partial(kernel, owners, slabs, capacity, rows_dev, width_cols),
        out_shape=jax.ShapeDtypeStruct((tokens_dev, channels), bf16),
        in_specs=[vmem] * 3 + [anywhere] * 5,
        out_specs=vmem,
        scratch_shapes=[
            pltpu.VMEM((model_width, hidden_units), bf16),
            pltpu.VMEM((hidden_units, model_width), bf16),
            pltpu.VMEM((model_width, channels), bf16),
            pltpu.VMEM((3, 3 * channels, channels), bf16),
            pltpu.VMEM((3, 3 * channels, channels), bf16),
            pltpu.VMEM((hidden_units, channels), bf16),
            pltpu.VMEM((tokens_dev, model_width), bf16),
            pltpu.VMEM((owners, capacity, model_width), bf16),
            pltpu.VMEM((owners, capacity, model_width), bf16),
            pltpu.VMEM((owners, capacity, channels), bf16),
            pltpu.VMEM((owners, capacity, channels), bf16),
            pltpu.VMEM((padded, channels), f32),
            pltpu.VMEM((padded + 2 * width_cols, channels), bf16),
            pltpu.VMEM((padded, channels), bf16),
            pltpu.VMEM((padded + 2 * width_cols, 3 * channels), bf16),
            pltpu.SemaphoreType.DMA((5,)),
            pltpu.SemaphoreType.DMA((owners,)),
            pltpu.SemaphoreType.DMA((owners,)),
            pltpu.SemaphoreType.DMA((owners,)),
            pltpu.SemaphoreType.DMA((owners,)),
            pltpu.SemaphoreType.DMA((2,)),
            pltpu.SemaphoreType.DMA((2,)),
        ],
        compiler_params=pltpu.CompilerParams(
            collective_id=0, has_side_effects=True, vmem_limit_bytes=56 * 2**20
        ),
    )(
        features.reshape(tokens_dev, model_width),
        codes,
        gates.reshape(tokens_dev, 2).T,
        w_in,
        w_out,
        w_proj,
        kernel_one.reshape(3, 3 * channels, channels),
        kernel_two.reshape(3, 3 * channels, channels),
    )
    return joined.reshape(maps_dev, rows_dev, width_cols, channels)


def solution(mesh):
    placed = (
        P("expert", "slab", None, None),
        P("expert", "slab", None, None),
        P("expert", "slab", None, None),
        P("expert", "slab", None, None),
        P("expert", None, None),
        P("expert", None, None),
        P(),
        P(),
        P(),
    )
    return jax.shard_map(
        functools.partial(shards, mesh.shape["expert"], mesh.shape["slab"]),
        mesh=mesh,
        in_specs=placed,
        out_specs=P("expert", "slab", None, None),
        check_vma=False,
    )
```
